32 devices in a mesh: row: 4 (over y, core), col: 8 (over z, x).
Axes of the slice: x: 2, y: 2, z: 4, core: 2. Of those that a mesh axis runs over, the one named last changes fastest.
Arguments:
- fisher: float32 [16384, 16384], P('row', 'col'), may hold values from -6 to 6
- slab: float32 [256, 16384], P(('row', 'col')), may hold values from -6 to 6
Outputs:
- fisher_out: float32 [16384, 16384], P('row', 'col')
The draws below stay inside these ranges and needn't reach their ends.
All inputs are finite; a program needn't handle non-finite values.
Results may differ from the reference program's by a relative error of at most 0.00005.
Values sent between devices are 32-bit elements; how exact they have to be, the bound alone decides.
A program may use at most 128 MiB of HBM per device.

```python
import jax
import jax.numpy as jnp
from jax import lax

ORDER = 16384
EXAMPLES = 256


def block_scale(stream_key, extent, shards, smallest, largest):
    factor_of, own = 1.0, jax.random.fold_in(stream_key, 6)
    for position, shards_of in shards:
        steps = jnp.exp(jax.random.uniform(jax.random.fold_in(own, position), (shards_of,), jnp.float32, smallest / len(shards), largest / len(shards)))
        factor_of = factor_of * jnp.repeat(steps, extent[position] // shards_of).reshape([-1 if axis == position else 1 for axis in range(len(extent))])
    return factor_of


def scatter_about(stream_key, extent, scale, most, cuts=(), kind=jnp.bfloat16):
    drawn = scale * jax.random.normal(stream_key, extent, jnp.float32)
    if cuts:
        drawn = drawn * block_scale(stream_key, extent, cuts, -0.22, 0.18)
    return jnp.clip(drawn, -most, most).astype(kind)


def setup_inputs(seed: int = 0) -> dict:
    keys = jax.random.split(jax.random.key(seed), 3)
    fisher = scatter_about(keys[0], (ORDER, ORDER), 1.0, 6.0, ((0, 4), (1, 8)), jnp.float32)
    slab = scatter_about(keys[1], (EXAMPLES, ORDER), 1.0, 6.0, ((0, 32),), jnp.float32)
    return dict(fisher=fisher, slab=slab)


def reference(fisher, slab):
    product = lax.dot_general(slab, slab, (((0,), (0,)), ((), ())), precision=lax.Precision.HIGHEST, preferred_element_type=jnp.float32)
    return fisher + product / EXAMPLES
```

```python
import functools

import jax
import jax.numpy as jnp
from jax import lax
from jax.experimental import pallas as pl
from jax.experimental.pallas import tpu as pltpu
from jax.sharding import PartitionSpec as P

MESH = pl.DeviceIdType.MESH


def gather_kernel(n_row, n_col, slab_ref, row_ref, col_ref, send_a, recv_a, send_g, recv_g, send_c, recv_c, local):
    t_row, t_col = row_ref.shape[3], col_ref.shape[3]
    r, c = lax.axis_index("row"), lax.axis_index("col")
    n_x = 2
    n_z = n_col // n_x
    z, x = c // n_x, c % n_x
    owner = c * t_col // t_row
    offset = pl.multiple_of(c * t_col - owner * t_row, t_col)
    sibling = r + 1 - 2 * (r % 2)
    leader = r % 2 == owner % 2
    is_owner = r == owner

    barrier = pltpu.get_barrier_semaphore()

    def greet_row(i, _):
        pl.semaphore_signal(barrier, inc=1, device_id=(lax.rem(r + i, n_row), c), device_id_type=MESH)
        return 0

    lax.fori_loop(1, n_row, greet_row, 0)
    has_up, has_down = z < n_z - 1, z > 0
    across = z * n_x + 1 - x
    pl.semaphore_signal(barrier, inc=1, device_id=(r, across), device_id_type=MESH)

    @pl.when(has_up)
    def _():
        pl.semaphore_signal(barrier, inc=1, device_id=(r, c + n_x), device_id_type=MESH)

    @pl.when(has_down)
    def _():
        pl.semaphore_signal(barrier, inc=1, device_id=(r, c - n_x), device_id_type=MESH)

    pl.semaphore_wait(barrier, n_row + has_up.astype(jnp.int32) + has_down.astype(jnp.int32))

    def tile(q):
        return slab_ref.at[:, pl.ds(pl.multiple_of(q * t_row, t_row), t_row)]

    def exchange(i):
        q = lax.rem(r + i, n_row)
        return pltpu.make_async_remote_copy(
            src_ref=tile(q), dst_ref=row_ref.at[c, r], send_sem=send_a.at[q], recv_sem=recv_a.at[r],
            device_id=(q, c), device_id_type=MESH)

    def arrival(q):
        return pltpu.make_async_remote_copy(
            src_ref=tile(q), dst_ref=row_ref.at[c, q], send_sem=send_a.at[q], recv_sem=recv_a.at[q],
            device_id=(q, c), device_id_type=MESH)

    def move(way, k, q):
        to = (c + n_x, c - n_x, across)[way]
        return pltpu.make_async_remote_copy(
            src_ref=row_ref.at[k, q], dst_ref=row_ref.at[k, q], send_sem=send_g.at[way, k, q], recv_sem=recv_g.at[k, q],
            device_id=(r, to), device_id_type=MESH)

    def spread(k, p):
        return pltpu.make_async_remote_copy(
            src_ref=row_ref.at[k, :, :, pl.ds(offset, t_col)], dst_ref=col_ref.at[k], send_sem=send_c.at[k, p],
            recv_sem=recv_c.at[k], device_id=(2 * p + owner % 2, c), device_id_type=MESH)

    def to_sibling(k):
        return pltpu.make_async_remote_copy(
            src_ref=col_ref.at[k], dst_ref=col_ref.at[k], send_sem=send_c.at[k, r // 2],
            recv_sem=recv_c.at[k], device_id=(sibling, c), device_id_type=MESH)

    def owner_to_sibling(k):
        return pltpu.make_async_remote_copy(
            src_ref=row_ref.at[k, :, :, pl.ds(offset, t_col)], dst_ref=col_ref.at[k], send_sem=send_c.at[k, r // 2],
            recv_sem=recv_c.at[k], device_id=(sibling, c), device_id_type=MESH)

    def own_columns(k):
        return pltpu.make_async_copy(row_ref.at[k, :, :, pl.ds(offset, t_col)], col_ref.at[k], recv_c.at[k])

    def for_pairs(what, k):
        def one(p, _):
            @pl.when(p != r // 2)
            def _():
                what(spread(k, p))
            return 0

        lax.fori_loop(0, n_row // 2, one, 0)

    def spread_block(k):
        @pl.when(is_owner)
        def _():
            for_pairs(lambda copy: copy.start(), k)
            owner_to_sibling(k).start()
            own_columns(k).start()

    def pass_on(k):
        @pl.when(leader & ~is_owner)
        def _():
            to_sibling(k).wait_recv()
            to_sibling(k).start()

    def exchange_one(i, _):
        exchange(i).start()
        return 0

    mine = pltpu.make_async_copy(tile(r), row_ref.at[c, r], local)
    mine.start()
    lax.fori_loop(1, n_row, exchange_one, 0)
    mine.wait()

    def send_own(i, _):
        q = lax.rem(r + n_row - i, n_row)

        @pl.when(i > 0)
        def _():
            arrival(q).wait_recv()

        @pl.when(has_up)
        def _():
            move(0, c, q).start()

        @pl.when(has_down)
        def _():
            move(1, c, q).start()

        move(2, c, q).start()
        return 0

    lax.fori_loop(0, n_row, send_own, 0)
    spread_block(c)

    def received(k):
        def one(i, _):
            move(2, k, lax.rem(r + n_row - i, n_row)).wait_recv()
            return 0

        lax.fori_loop(0, n_row, one, 0)

    def crossed(s):
        for k, there in ((across - s * n_x, z >= s), (across + s * n_x, z + s < n_z)):
            if s == 0 and k is not None:
                there = True

            def both(k=k):
                received(k)
                spread_block(k)

            if s == 0:
                both()
                return
            pl.when(there)(both)

    def passed(s):
        if s == 0:
            pass_on(c)
            pass_on(across)
            return
        for k, there in ((c - s * n_x, z >= s), (c + s * n_x, z + s < n_z)):
            def both(k=k):
                pass_on(k)
                pass_on(k + 1 - 2 * x)

            pl.when(there)(both)

    for s in range(1, n_z):
        def step(i, _, s=s):
            q = lax.rem(r + n_row - i, n_row)

            @pl.when(z >= s)
            def _():
                k = c - s * n_x
                move(0, k, q).wait_recv()

                @pl.when(has_up)
                def _():
                    move(0, k, q).start()

                move(2, k, q).start()

            @pl.when(z + s < n_z)
            def _():
                k = c + s * n_x
                move(1, k, q).wait_recv()

                @pl.when(has_down)
                def _():
                    move(1, k, q).start()

                move(2, k, q).start()
            return 0

        lax.fori_loop(0, n_row, step, 0)
        for k, there in ((c - s * n_x, z >= s), (c + s * n_x, z + s < n_z)):
            pl.when(there)(functools.partial(spread_block, k))
        if s >= 2:
            crossed(s - 2)
            passed(s - 2)
    for s in range(max(n_z - 2, 0), n_z):
        crossed(s)
    for s in range(max(n_z - 2, 0), n_z):
        passed(s)

    def sent_own(i, _):
        exchange(i).wait_send()
        return 0

    lax.fori_loop(1, n_row, sent_own, 0)

    def finish(k, _):
        same = k % n_x == x

        def one(q, _):
            @pl.when(same)
            def _():
                move(2, k, q).wait_send()

            @pl.when(same & has_up & (k <= c))
            def _():
                move(0, k, q).wait_send()

            @pl.when(same & has_down & (k >= c))
            def _():
                move(1, k, q).wait_send()
            return 0

        lax.fori_loop(0, n_row, one, 0)

        @pl.when(is_owner)
        def _():
            for_pairs(lambda copy: copy.wait_send(), k)
            owner_to_sibling(k).wait_send()
            own_columns(k).wait()

        @pl.when(leader & ~is_owner)
        def _():
            to_sibling(k).wait_send()

        @pl.when(~leader)
        def _():
            to_sibling(k).wait_recv()
        return 0

    lax.fori_loop(0, n_col, finish, 0)


def gather(slab, n_row, n_col, t_row, t_col):
    rows = slab.shape[0]
    dma = pltpu.SemaphoreType.DMA
    return pl.pallas_call(
        functools.partial(gather_kernel, n_row, n_col),
        out_shape=(
            jax.ShapeDtypeStruct((n_col, n_row, rows, t_row), jnp.float32),
            jax.ShapeDtypeStruct((n_col, n_row, rows, t_col), jnp.float32),
        ),
        in_specs=[pl.BlockSpec(memory_space=pl.ANY)],
        out_specs=(pl.BlockSpec(memory_space=pl.ANY),) * 2,
        scratch_shapes=[
            dma((n_row,)), dma((n_row,)), dma((3, n_col, n_row)), dma((n_col, n_row)),
            dma((n_col, n_row // 2)), dma((n_col,)), dma(()),
        ],
        compiler_params=pltpu.CompilerParams(collective_id=0, has_side_effects=True),
        name="gather_panels",
    )(slab)


def split(values):
    high = values.astype(jnp.bfloat16)
    low = (values - high.astype(jnp.float32)).astype(jnp.bfloat16)
    return high, low


def add_kernel(examples, fisher_ref, left_ref, right_ref, out_ref, split_right):
    depth = right_ref.shape[0]

    @pl.when(pl.program_id(0) == 0)
    def _():
        high, low = split(right_ref[...])
        split_right[0:depth] = high
        split_right[depth : 2 * depth] = low
        split_right[2 * depth :] = high

    high, low = split(left_ref[...])
    left = jnp.concatenate([high, high, low], axis=0)
    product = lax.dot_general(
        left, split_right[...], (((0,), (0,)), ((), ())), preferred_element_type=jnp.float32
    )
    out_ref[...] = fisher_ref[...] + product * (1.0 / examples)


def add_product(fisher, left, right, examples):
    t_row, t_col = fisher.shape
    tile = min(512, t_row)
    depth = left.shape[0]
    return pl.pallas_call(
        functools.partial(add_kernel, examples),
        grid=(t_row // tile,),
        out_shape=jax.ShapeDtypeStruct(fisher.shape, fisher.dtype),
        in_specs=[
            pl.BlockSpec((tile, t_col), lambda i: (i, 0)),
            pl.BlockSpec((depth, tile), lambda i: (0, i)),
            pl.BlockSpec((depth, t_col), lambda i: (0, 0)),
        ],
        out_specs=pl.BlockSpec((tile, t_col), lambda i: (i, 0)),
        scratch_shapes=[pltpu.VMEM((3 * depth, t_col), jnp.bfloat16)],
        compiler_params=pltpu.CompilerParams(vmem_limit_bytes=56 * 2**20),
        cost_estimate=pl.CostEstimate(
            flops=6 * depth * t_row * t_col, bytes_accessed=8 * t_row * t_col, transcendentals=0
        ),
        name="add_product",
    )(fisher, left, right)


def body(fisher, slab):
    n_row = lax.axis_size("row")
    n_col = lax.axis_size("col")
    rows, order = slab.shape
    t_row = order // n_row
    t_col = order // n_col
    examples = rows * n_row * n_col
    left, right = gather(slab, n_row, n_col, t_row, t_col)
    return add_product(fisher, left.reshape(examples, t_row), right.reshape(examples, t_col), examples)


def solution(mesh):
    return jax.shard_map(
        body,
        mesh=mesh,
        in_specs=(P("row", "col"), P(("row", "col"), None)),
        out_specs=P("row", "col"),
        check_vma=False,
    )
```
